32 devices in a mesh: dp: 2 (over y), band: 16 (over z, x, core).
Axes of the slice: x: 2, y: 2, z: 4, core: 2. Of those that a mesh axis runs over, the one named last changes fastest.
Arguments:
- grad_out: bfloat16 [2, 16, 128, 1024], P('dp', None, 'band'), may hold values from -6 to 6
- features: bfloat16 [2, 32, 128, 1024], P('dp', None, 'band'), may hold values from -6 to 6
- conv_weight: bfloat16 [3, 3, 16, 32], replicated, may hold values from -0.5 to 0.5
- block_weights: bfloat16 [1536, 128, 128], P('band'), may hold values from 0 to 0.049804688
- fine_tile: int32 [1536], P('band'), may hold values from 0 to 63
- coarse_tile: int32 [1536], P('band'), may hold values from 0 to 95, as said below
- owner_slot: int32 [96], replicated, may hold values from 0 to 95, as said below
- send_counts: int32 [16, 16], P('band'), may hold values from 0 to 12, as said below
Outputs:
- grad_features: bfloat16 [2, 32, 128, 1024], P('dp', None, 'band')
- conv_grad: float32 [3, 3, 16, 32], replicated
- coarse_grad: float32 [2, 96, 16, 128], P('dp', 'band')
The draws below stay inside these ranges and needn't reach their ends.
Inputs may be any that keep to these rules, and one draw needn't show every extreme that they name: `send_counts`: row b names, for each owner, how many of band b's first blocks have coarse tiles that this owner holds; one owner gets exactly 12 from every band; a row sums to between 48 and 96, and to 96 in some band. `coarse_tile`: the live blocks of a band are ordered by owner as send_counts gives: those of owner 0 first, then those of owner 1, and so on. `owner_slot`: each value once; coarse tile t is held by band owner_slot[t] // 6 at place owner_slot[t] % 6.
All inputs are finite; a program needn't handle non-finite values.
Results may differ from the reference program's by a relative error of at most 0.005.
Values may be sent and summed in bfloat16 or wider, within the bound.
A program may use at most 64 MiB of HBM per device.

```python
import math
import jax
import jax.numpy as jnp
from jax import lax

CH = 16
CIN = 32
TILE = 128
COLS = 1024
FT = 64
NB = 96
CAP = 12
CT_DEV = 6
CT_ALL = 96
NBLK = 1536
NLAT = 128
SAMPLES = 2
N_BAND = 16


def counts_table(key):
    hot_owner = jax.random.randint(jax.random.fold_in(key, 11), (), 0, N_BAND)
    full_band = jax.random.randint(jax.random.fold_in(key, 12), (), 0, N_BAND)
    lower = max(CAP, NB // 2)
    live_total = jax.random.randint(jax.random.fold_in(key, 13), (N_BAND,), lower, NB + 1)
    live_total = jnp.where(jnp.arange(N_BAND) == full_band, NB, live_total).astype(jnp.int32)

    def one_row(row_key, total):
        order_perm = jax.random.permutation(row_key, (N_BAND - 1) * CAP).astype(jnp.int32)
        units = jnp.arange(N_BAND * CAP, dtype=jnp.int32)
        owner = units // CAP
        other = jnp.where(owner < hot_owner, units, units - CAP)
        other = jnp.clip(other, 0, (N_BAND - 1) * CAP - 1)
        ranked = order_perm[other]
        taken = (owner == hot_owner) | (ranked < total - CAP)
        return jnp.sum(taken.reshape(N_BAND, CAP).astype(jnp.int32), axis=1)
    row_keys = jax.random.split(jax.random.fold_in(key, 14), N_BAND)
    return jax.vmap(one_row)(row_keys, live_total).astype(jnp.int32)


def slot_table(key):
    return jax.random.permutation(jax.random.fold_in(key, 21), CT_ALL).astype(jnp.int32)


def draw_send_counts(key, part):
    return counts_table(key)


def draw_owner_slot(key, part):
    return slot_table(key)


def draw_coarse_tile(key, part):
    tallies = counts_table(key)
    owner_slot = slot_table(key)
    tile_of_slot = jnp.argsort(owner_slot).astype(jnp.int32)
    running = jnp.cumsum(tallies, axis=1)
    position = jnp.arange(NB, dtype=jnp.int32)
    owner = jnp.sum((running[:, None, :] <= position[None, :, None]).astype(jnp.int32), axis=2)
    owner = jnp.clip(owner, 0, N_BAND - 1)
    place = jax.random.randint(jax.random.fold_in(key, 22), (N_BAND, NB), 0, CT_DEV)
    slots = owner * CT_DEV + place
    return tile_of_slot[slots].reshape(-1).astype(jnp.int32)


def plant(result, rng, low, high):
    dims = result.shape
    index_at = [jax.random.randint(jax.random.fold_in(rng, axis), (), 0, dims[axis]) for axis in range(len(dims))]
    result = result.at[tuple(index_at)].set(low)
    longest = dims.index(max(dims))
    index_at[longest] = (index_at[longest] + 1) % dims[longest]
    return result.at[tuple(index_at)].set(high)


def steps_of(key, shape, cuts, low, top_value):
    level, own = 1.0, jax.random.fold_in(key, 6)
    for dim, parts in cuts:
        heights = jnp.exp(jax.random.uniform(jax.random.fold_in(own, dim), (parts,), jnp.float32, low / len(cuts), top_value / len(cuts)))
        level = level * jnp.repeat(heights, shape[dim] // parts).reshape([-1 if axis == dim else 1 for axis in range(len(shape))])
    return level


def bell_draw(key, dims, scale, limit, cuts=(), kind=jnp.bfloat16):
    result = jax.random.normal(key, dims, jnp.float32) * scale
    if len(cuts) > 0:
        result = steps_of(key, dims, cuts, -0.22, 0.18) * result
    return jnp.clip(result, min=-limit, max=limit).astype(kind)


def setup_inputs(seed: int = 0) -> dict:
    streams_of = jax.random.split(jax.random.key(seed), 9)
    return {
        "grad_out": bell_draw(streams_of[0], (SAMPLES, CH, NLAT, COLS), 1.0, 6.0, ((0, 2), (2, 16))),
        "features": bell_draw(streams_of[1], (SAMPLES, CIN, NLAT, COLS), 1.0, 6.0, ((0, 2), (2, 16))),
        "conv_weight": bell_draw(streams_of[2], (3, 3, CH, CIN), (9 * CH) ** -0.5, 0.5),
        "block_weights": jnp.clip(0.049804688 * jax.random.uniform(streams_of[3], (NBLK, TILE, TILE), jnp.float32) ** steps_of(streams_of[3], (NBLK, TILE, TILE), ((0, 16),), -0.2, 0.2), 0.0, 0.049804688).astype(jnp.bfloat16),
        "fine_tile": plant(jax.random.randint(streams_of[4], (NBLK,), 0, FT), jax.random.fold_in(streams_of[4], 1), 0, FT - 1).astype(jnp.int32),
        "coarse_tile": draw_coarse_tile(jax.random.fold_in(streams_of[8], 71), 0),
        "owner_slot": draw_owner_slot(jax.random.fold_in(streams_of[8], 71), 0),
        "send_counts": draw_send_counts(jax.random.fold_in(streams_of[8], 71), 0),
    }


def reference(grad_out, features, conv_weight, block_weights, fine_tile, coarse_tile, owner_slot, send_counts):
    weights_wide = block_weights.astype(jnp.float32)
    block_ids = jnp.arange(NBLK, dtype=jnp.int32)
    band_of = block_ids // NB
    live_count = lax.optimization_barrier(jnp.sum(send_counts, axis=1)).astype(jnp.int32)
    in_use = (block_ids % NB < live_count[band_of]).astype(jnp.float32)
    fine_id = (band_of * FT + fine_tile).astype(jnp.int32)
    slot_of = owner_slot[coarse_tile].astype(jnp.int32)

    def one_sample(cotangent):
        tiles_wide = cotangent.reshape(CH, N_BAND * FT, TILE).astype(jnp.float32)
        picked = tiles_wide[:, fine_id, :]
        partial_value = jnp.einsum('cbi,bij->bcj', picked, weights_wide, precision=lax.Precision.HIGHEST)
        partial_value = partial_value * in_use[:, None, None]
        coarse = jax.ops.segment_sum(partial_value, slot_of, num_segments=CT_ALL)
        returned = coarse[slot_of] * in_use[:, None, None]
        spread = jnp.einsum('bcj,bij->bci', returned, weights_wide, precision=lax.Precision.HIGHEST)
        correction = jax.ops.segment_sum(spread, fine_id, num_segments=N_BAND * FT)
        correction = jnp.transpose(correction, (1, 0, 2)).reshape(CH, NLAT, COLS)
        grad_mid = (cotangent.astype(jnp.float32) - correction).astype(jnp.bfloat16)
        return (coarse, grad_mid)
    coarse_grad, grad_mid = lax.map(one_sample, grad_out)
    kernel = conv_weight.astype(jnp.float32)
    scaling = 1.0 / math.sqrt(SAMPLES * NLAT * COLS)

    def conv_sample(pair):
        middle, inputs = pair
        padded_mid = jnp.pad(middle.astype(jnp.float32), ((0, 0), (1, 1), (1, 1)))
        padded_in = jnp.pad(inputs.astype(jnp.float32), ((0, 0), (1, 1), (1, 1)))
        middle_wide = middle.astype(jnp.float32)
        total = jnp.zeros((CIN, NLAT, COLS), jnp.float32)
        rows_of_kernel = []
        for row_shift in range(3):
            cols_of_kernel = []
            for col_shift in range(3):
                window_mid = padded_mid[:, 2 - row_shift:2 - row_shift + NLAT, 2 - col_shift:2 - col_shift + COLS]
                total = total + jnp.einsum('ki,krq->irq', kernel[row_shift, col_shift], window_mid, precision=lax.Precision.HIGHEST)
                window_in = padded_in[:, row_shift:row_shift + NLAT, col_shift:col_shift + COLS]
                cols_of_kernel.append(jnp.einsum('krq,irq->ki', middle_wide, window_in, precision=lax.Precision.HIGHEST))
            rows_of_kernel.append(jnp.stack(cols_of_kernel))
        return (total.astype(jnp.bfloat16), jnp.stack(rows_of_kernel))
    grad_features, kernel_terms = lax.map(conv_sample, (grad_mid, features))
    conv_grad = lax.optimization_barrier(jnp.sum(kernel_terms, axis=0)) * scaling
    return (grad_features, conv_grad, coarse_grad)
```

```python
import functools
import math

import jax
import jax.numpy as jnp
from jax import lax
from jax.experimental import pallas as pl
from jax.experimental.pallas import tpu as pltpu
from jax.sharding import PartitionSpec as P

F32 = jnp.float32
BF16 = jnp.bfloat16
MESH = pl.DeviceIdType.MESH
NT = (((1,), (1,)), ((), ()))


def split_bf16(value):
    high = value.astype(BF16)
    low = (value - high.astype(F32)).astype(BF16)
    return high, low


def kernel(
    dims,
    ft_s,
    ct_s,
    os_s,
    ft_v,
    ct_v,
    os_v,
    sc_v,
    go,
    feat,
    cw,
    weights,
    gf_out,
    cg_out,
    co_out,
    stage,
    tiles,
    terms,
    sums,
    tx1,
    rx1,
    tx2,
    rx2,
    back,
    corr,
    comb,
    featr,
    edges,
    halo,
    ar1,
    ar2,
    ar3,
    s1s,
    s1r,
    s2s,
    s2r,
    gos,
    gis,
    grs,
    hs,
    hr,
    a1s,
    a1r,
    a2s,
    a2r,
    a3s,
    a3r,
):
    n_dp, bands, n1, n2, channels, cin, rows, cols, tl, nb, per, ct_all, scaling = dims
    cblocks = cols // tl
    n_tiles = rows * cblocks
    group = n2 * per
    me = lax.axis_index("band")
    my_dp = lax.axis_index("dp")
    my_o = me // n1
    my_i = me % n1

    barrier = pltpu.get_barrier_semaphore()

    def inner(i):
        return {"band": my_o * n1 + i}

    def outer(z):
        return {"band": z * n1 + my_i}

    def greet(device):
        pl.semaphore_signal(barrier, inc=1, device_id=device, device_id_type=MESH)

    for d in range(1, n1):
        greet(inner((my_i + d) % n1))
    for e in range(1, n2):
        greet(outer((my_o + e) % n2))
    for f in range(1, n_dp):
        greet({"dp": (my_dp + f) % n_dp})

    @pl.when(me > 0)
    def _():
        greet({"band": me - 1})

    @pl.when(me < bands - 1)
    def _():
        greet({"band": me + 1})

    for b in range(cblocks):
        part = go[:, :, b * tl : (b + 1) * tl].astype(F32)
        stage[b, 0 : channels * rows, :] = part.reshape(channels * rows, tl)
        for r in range(rows):
            line = stage[b, pl.ds(r, channels, stride=rows), :]
            tiles[r * cblocks + b] = line.astype(BF16)

    step = 8

    def forward(t, carry):
        for a in range(step):
            k = t * step + a
            product = jnp.dot(tiles[ft_s[k]], weights[k], preferred_element_type=F32)
            terms[pl.ds(pl.multiple_of(k * channels, channels), channels), :] = product
        return carry

    lax.fori_loop(0, nb // step, forward, 0)

    def owner_parts(slot):
        owner = lax.shift_right_logical(slot * (65536 // per + 1), 16)
        place = slot - owner * per
        z = lax.shift_right_logical(owner, n1.bit_length() - 1)
        i = owner & (n1 - 1)
        return (i * n2 + z) * per + place

    live = jnp.sum(sc_v[...], axis=1, keepdims=True)
    in_use = lax.broadcasted_iota(jnp.int32, (1, nb), 1) < live
    eye = lax.broadcasted_iota(jnp.int32, (ct_all, ct_all), 0) == lax.broadcasted_iota(
        jnp.int32, (ct_all, ct_all), 1
    )
    row_of = owner_parts(os_v[...])
    column = jnp.sum(jnp.where(eye, row_of, 0), axis=1, keepdims=True)
    match = lax.broadcasted_iota(jnp.int32, (ct_all, nb), 0) == ct_v[...]
    row_of_block = jnp.sum(jnp.where(match, column, 0), axis=0, keepdims=True)
    row_of_block = jnp.where(in_use, row_of_block, -1)
    select = (lax.broadcasted_iota(jnp.int32, (ct_all, nb), 0) == row_of_block).astype(F32)
    select = jnp.concatenate([select.astype(BF16)] * 2, axis=1)
    fine = jnp.where(in_use, ft_v[...], -1)
    pick = (lax.broadcasted_iota(jnp.int32, (n_tiles, nb), 0) == fine).astype(F32)
    pick = jnp.concatenate([pick.astype(BF16)] * 2, axis=1)

    def gather_sum(chooser, target, count):
        for c in range(0, channels, 2):
            parts = [terms[pl.ds(c + a, nb, stride=channels), :] for a in range(2)]
            high, low = split_bf16(jnp.concatenate(parts, axis=1))
            both = jnp.concatenate([high, low], axis=0)
            total = jnp.dot(chooser, both, preferred_element_type=F32)
            for a in range(2):
                target[pl.ds(c + a, count, stride=channels), :] = total[:, a * tl : (a + 1) * tl]

    gather_sum(select, sums, ct_all)
    tx1[...] = sums[...].astype(BF16).reshape(ct_all, channels, tl)

    peers = (n1 - 1) + (n2 - 1) + (n_dp - 1)
    peers = peers + jnp.minimum(me, 1) + jnp.minimum(bands - 1 - me, 1)
    pl.semaphore_wait(barrier, peers)

    def remote(src, dst, send, recv, device):
        return pltpu.make_async_remote_copy(
            src_ref=src,
            dst_ref=dst,
            send_sem=send,
            recv_sem=recv,
            device_id=device,
            device_id_type=MESH,
        )

    first = []
    for d in range(1, n1):
        to = (my_i + d) % n1
        copy = remote(
            tx1.at[pl.ds(to * group, group)], rx1.at[d - 1], s1s.at[d - 1], s1r.at[d - 1], inner(to)
        )
        copy.start()
        first.append(copy)

    for b in range(cblocks):
        part = feat[:, :, b * tl : (b + 1) * tl].astype(F32)
        stage[b] = part.reshape(cin * rows, tl)
        for r in range(rows):
            line = stage[b, pl.ds(r, cin, stride=rows), :]
            featr[r, :, b * tl : (b + 1) * tl] = line.astype(BF16)
    slab = 3 * channels
    kernel_rows = jnp.concatenate([cw[(2 - p) * slab : (3 - p) * slab, :] for p in range(3)], axis=0)
    kernel_t = kernel_rows.astype(F32).T.astype(BF16)

    for copy in first:
        copy.wait()

    size = per * channels

    def inner_sum(z):
        own = sums[pl.ds(pl.multiple_of((my_i * group + z * per) * channels, size), size), :]
        for d in range(n1 - 1):
            own = own + rx1[d, pl.ds(z * per, per)].astype(F32).reshape(size, tl)
        return own

    second = []
    for e in range(1, n2):
        to = (my_o + e) % n2
        tx2[e - 1] = inner_sum(to).astype(BF16).reshape(per, channels, tl)
        copy = remote(tx2.at[e - 1], rx2.at[e - 1], s2s.at[e - 1], s2r.at[e - 1], outer(to))
        copy.start()
        second.append(copy)
    owned = inner_sum(my_o)
    for e in range(1, n2):
        second[e - 1].wait()
        owned = owned + rx2[e - 1].astype(F32).reshape(size, tl)

    def place(i, z):
        return back.at[pl.ds((i * n2 + z) * per, per)]

    back[pl.ds((my_i * n2 + my_o) * per, per)] = owned.astype(BF16).reshape(per, channels, tl)

    sent = []

    def pass_on(z, e):
        here = place(my_i, z)
        for d in range(1, n1):
            copy = remote(
                here, here, gis.at[d - 1, e], grs.at[my_i, z], inner((my_i + d) % n1)
            )
            copy.start()
            sent.append(copy)

    mine = place(my_i, my_o)
    for e in range(1, n2):
        copy = remote(mine, mine, gos.at[e - 1], grs.at[my_i, my_o], outer((my_o + e) % n2))
        copy.start()
        sent.append(copy)
    pass_on(my_o, 0)
    co_out[...] = owned.reshape(per, channels, tl)
    for e in range(1, n2):
        z = (my_o + n2 - e) % n2
        here = place(my_i, z)
        remote(here, here, gos.at[e - 1], grs.at[my_i, z], outer(z)).wait_recv()
        pass_on(z, e)
    for d in range(1, n1):
        i = (my_i + d) % n1
        for e in range(n2):
            z = (my_o + n2 - e) % n2
            here = place(i, z)
            remote(here, here, gis.at[d - 1, e], grs.at[i, z], inner(i)).wait_recv()
    for copy in sent:
        copy.wait_send()

    def row_index(slot):
        owner = slot // per
        return ((owner % n1) * n2 + owner // n1) * per + slot % per

    def backward(t, carry):
        for a in range(step):
            k = t * step + a
            value = back[row_index(os_s[ct_s[k]])]
            product = lax.dot_general(value, weights[k], NT, preferred_element_type=F32)
            terms[pl.ds(pl.multiple_of(k * channels, channels), channels), :] = product
        return carry

    lax.fori_loop(0, nb // step, backward, 0)
    gather_sum(pick, corr, n_tiles)

    col = lax.broadcasted_iota(jnp.int32, (channels, cols), 1)

    def mid_row(r):
        parts = []
        for b in range(cblocks):
            g = r * cblocks + b
            parts.append(tiles[g].astype(F32) - corr[g * channels : (g + 1) * channels, :])
        return jnp.concatenate(parts, axis=1).astype(BF16)

    def put_row(p, line):
        wide = line.astype(F32)
        later = jnp.where(col == cols - 1, 0.0, pltpu.roll(wide, cols - 1, 1))
        earlier = jnp.where(col == 0, 0.0, pltpu.roll(wide, 1, 1))
        comb[p * slab : p * slab + channels, :] = later.astype(BF16)
        comb[p * slab + channels : p * slab + 2 * channels, :] = line
        comb[p * slab + 2 * channels : (p + 1) * slab, :] = earlier.astype(BF16)

    top, bottom = mid_row(0), mid_row(rows - 1)
    edges[0] = top
    edges[1] = bottom
    up = remote(edges.at[0], halo.at[1], hs.at[0], hr.at[1], {"band": jnp.maximum(me - 1, 0)})
    down = remote(
        edges.at[1], halo.at[0], hs.at[1], hr.at[0], {"band": jnp.minimum(me + 1, bands - 1)}
    )

    @pl.when(me > 0)
    def _():
        up.start()

    @pl.when(me < bands - 1)
    def _():
        down.start()

    put_row(1, top)
    put_row(rows, bottom)
    for r in range(1, rows - 1):
        put_row(r + 1, mid_row(r))

    def conv_row(r, total):
        window = comb[r * slab : (r + 3) * slab, :]
        result = jnp.dot(kernel_t, window, preferred_element_type=F32)
        for b in range(cblocks):
            stage[b, pl.ds(r, cin, stride=rows), :] = result[:, b * tl : (b + 1) * tl]
        return total + lax.dot_general(window, featr[r], NT, preferred_element_type=F32)

    total = jnp.zeros((3 * slab, cin), F32)
    for r in range(1, rows - 1):
        total = conv_row(r, total)

    @pl.when(me > 0)
    def _():
        down.wait_recv()
        put_row(0, halo[0])

    @pl.when(me == 0)
    def _():
        comb[0:slab, :] = jnp.zeros((slab, cols), BF16)

    @pl.when(me < bands - 1)
    def _():
        up.wait_recv()
        put_row(rows + 1, halo[1])

    @pl.when(me == bands - 1)
    def _():
        comb[(rows + 1) * slab : (rows + 2) * slab, :] = jnp.zeros((slab, cols), BF16)

    total = conv_row(0, total)
    total = conv_row(rows - 1, total)

    total = total * scaling
    packs = 128 // cin
    lines = ar1.shape[1]
    full = jnp.concatenate([total, jnp.zeros((packs * lines - 3 * slab, cin), F32)], axis=0)
    packed = jnp.concatenate([full[a * lines : (a + 1) * lines] for a in range(packs)], axis=1)

    def exchange(value, buf, send, recv, count, index, device):
        buf[index] = value
        copies = []
        for d in range(1, count):
            copy = remote(
                buf.at[index],
                buf.at[index],
                send.at[d - 1],
                recv.at[index],
                device((index + d) % count),
            )
            copy.start()
            copies.append(copy)

        def finish():
            for d in range(1, count):
                source = (index + d) % count
                remote(
                    buf.at[source], buf.at[source], send.at[d - 1], recv.at[source], device(source)
                ).wait_recv()
            for copy in copies:
                copy.wait_send()
            result = buf[0]
            for m in range(1, count):
                result = result + buf[m]
            return result

        return finish

    finish = exchange(packed, ar1, a1s, a1r, n1, my_i, inner)
    for b in range(cblocks):
        part = stage[b].reshape(cin, rows, tl)
        gf_out[:, :, b * tl : (b + 1) * tl] = part.astype(BF16)
    packed = finish()
    packed = exchange(packed, ar2, a2s, a2r, n2, my_o, outer)()
    packed = exchange(packed, ar3, a3s, a3r, n_dp, my_dp, lambda y: {"dp": y})()
    for u in range(3):
        for s in range((2 - u) * slab, (3 - u) * slab, 8):
            a, b = s // lines, s % lines
            at = u * slab + s - (2 - u) * slab
            cg_out[at : at + 8, :] = packed[b : b + 8, a * cin : (a + 1) * cin]

    @pl.when(me > 0)
    def _():
        up.wait_send()

    @pl.when(me < bands - 1)
    def _():
        down.wait_send()


def per_device(
    n_dp,
    bands,
    grad_out,
    features,
    conv_weight,
    block_weights,
    fine_tile,
    coarse_tile,
    owner_slot,
    send_counts,
):
    channels, rows, cols = grad_out.shape[1:]
    cin = features.shape[1]
    nb, tl = block_weights.shape[:2]
    ct_all = owner_slot.shape[0]
    per = ct_all // bands
    n1 = 4
    n2 = bands // n1
    n_tiles = rows * cols // tl
    scaling = 1.0 / math.sqrt(n_dp * bands * rows * cols)
    dims = (n_dp, bands, n1, n2, channels, cin, rows, cols, tl, nb, per, ct_all, scaling)
    slab = 3 * channels
    packs = 128 // cin
    lines = -(-3 * slab // (packs * 8)) * 8
    group = n2 * per
    dma = pltpu.SemaphoreType.DMA
    vmem = pl.BlockSpec(memory_space=pltpu.VMEM)
    smem = pl.BlockSpec(memory_space=pltpu.SMEM)
    gf, cg, co = pl.pallas_call(
        functools.partial(kernel, dims),
        out_shape=(
            jax.ShapeDtypeStruct((cin, rows, cols), BF16),
            jax.ShapeDtypeStruct((3 * slab, cin), F32),
            jax.ShapeDtypeStruct((per, channels, tl), F32),
        ),
        in_specs=[smem] * 3 + [vmem] * 8,
        out_specs=(vmem, vmem, vmem),
        scratch_shapes=[
            pltpu.VMEM((cols // tl, cin * rows, tl), F32),
            pltpu.VMEM((n_tiles, channels, tl), BF16),
            pltpu.VMEM((nb * channels, tl), F32),
            pltpu.VMEM((ct_all * channels, tl), F32),
            pltpu.VMEM((ct_all, channels, tl), BF16),
            pltpu.VMEM((n1 - 1, group, channels, tl), BF16),
            pltpu.VMEM((n2 - 1, per, channels, tl), BF16),
            pltpu.VMEM((n2 - 1, per, channels, tl), BF16),
            pltpu.VMEM((ct_all, channels, tl), BF16),
            pltpu.VMEM((n_tiles * channels, tl), F32),
            pltpu.VMEM(((rows + 2) * slab, cols), BF16),
            pltpu.VMEM((rows, cin, cols), BF16),
            pltpu.VMEM((2, channels, cols), BF16),
            pltpu.VMEM((2, channels, cols), BF16),
            pltpu.VMEM((n1, lines, 128), F32),
            pltpu.VMEM((n2, lines, 128), F32),
            pltpu.VMEM((n_dp, lines, 128), F32),
            dma((n1 - 1,)),
            dma((n1 - 1,)),
            dma((n2 - 1,)),
            dma((n2 - 1,)),
            dma((n2 - 1,)),
            dma((n1 - 1, n2)),
            dma((n1, n2)),
            dma((2,)),
            dma((2,)),
            dma((n1 - 1,)),
            dma((n1,)),
            dma((n2 - 1,)),
            dma((n2,)),
            dma((n_dp - 1,)),
            dma((n_dp,)),
        ],
        compiler_params=pltpu.CompilerParams(
            collective_id=0, has_side_effects=True, vmem_limit_bytes=48 * 1024 * 1024
        ),
    )(
        fine_tile,
        coarse_tile,
        owner_slot,
        fine_tile.reshape(1, nb),
        coarse_tile.reshape(1, nb),
        owner_slot.reshape(1, ct_all),
        send_counts,
        grad_out.reshape(channels, rows, cols),
        features.reshape(cin, rows, cols),
        conv_weight.reshape(3 * slab, cin),
        block_weights,
    )
    return gf[None], cg.reshape(3, 3, channels, cin), co[None]


def solution(mesh):
    placed = (
        P("dp", None, "band", None),
        P("dp", None, "band", None),
        P(),
        P("band", None, None),
        P("band"),
        P("band"),
        P(),
        P("band", None),
    )
    return jax.shard_map(
        functools.partial(per_device, mesh.shape["dp"], mesh.shape["band"]),
        mesh=mesh,
        in_specs=placed,
        out_specs=(P("dp", None, "band", None), P(), P("dp", "band", None, None)),
        check_vma=False,
    )
```

```python
import functools
import math

import jax
import jax.numpy as jnp
from jax import lax
from jax.experimental import pallas as pl
from jax.experimental.pallas import tpu as pltpu
from jax.sharding import PartitionSpec as P

F32 = jnp.float32
BF16 = jnp.bfloat16
MESH = pl.DeviceIdType.MESH
NT = (((1,), (1,)), ((), ()))


def split_bf16(value):
    high = value.astype(BF16)
    low = (value - high.astype(F32)).astype(BF16)
    return high, low


def kernel(
    dims,
    ft_h,
    ct_h,
    os_h,
    sc_h,
    go_h,
    feat_h,
    cw_h,
    weights_h,
    gf_out,
    cg_out,
    co_out,
    stage,
    tiles,
    terms,
    sums,
    tx1,
    rx1,
    tx2,
    rx2,
    back,
    corr,
    comb,
    featr,
    edges,
    halo,
    ar1,
    ar2,
    weights,
    weights_t,
    go,
    feat,
    cw,
    ft_s,
    ct_s,
    os_s,
    ft_v,
    ct_v,
    os_v,
    sc_v,
    loads,
    wloads,
    fhs,
    fhr,
    s1s,
    s1r,
    s2s,
    s2r,
    gos,
    gis,
    grs,
    hs,
    hr,
    a1s,
    a1r,
    a2s,
    a2r,
):
    n_dp, bands, n1, n2, channels, cin, rows, cols, tl, nb, per, ct_all, scaling = dims
    cblocks = cols // tl
    n_tiles = rows * cblocks
    group = n2 * per
    me = lax.axis_index("band")
    my_dp = lax.axis_index("dp")
    my_o = me // n1
    my_i = me % n1

    barrier = pltpu.get_barrier_semaphore()

    def inner(i):
        return {"band": my_o * n1 + i}

    def outer(z):
        return {"band": z * n1 + my_i}

    def greet(device):
        pl.semaphore_signal(barrier, inc=1, device_id=device, device_id_type=MESH)

    plane_count = n1 * n_dp
    my_p = my_dp * n1 + my_i

    def plane(p):
        return {"dp": p // n1, "band": my_o * n1 + p % n1}

    for d in range(1, plane_count):
        greet(plane((my_p + d) % plane_count))
    for e in range(1, n2):
        greet(outer((my_o + e) % n2))

    @pl.when(me > 0)
    def _():
        greet({"band": me - 1})

    @pl.when(me < bands - 1)
    def _():
        greet({"band": me + 1})

    ins = []
    for n, (src, dst) in enumerate(
        [
            (go_h, go),
            (ft_h, ft_s),
            (ct_h, ct_s),
            (os_h, os_s),
            (ft_h, ft_v),
            (ct_h, ct_v),
            (os_h, os_v),
            (sc_h, sc_v),
            (feat_h, feat),
            (cw_h, cw),
        ]
    ):
        ins.append(pltpu.make_async_copy(src, dst, loads.at[n]))
    w_chunks = wloads.shape[0]
    w_len = nb // w_chunks
    w_ins = [
        pltpu.make_async_copy(
            weights_h.at[pl.ds(n * w_len, w_len)], weights.at[pl.ds(n * w_len, w_len)], wloads.at[n]
        )
        for n in range(w_chunks)
    ]
    for copy in ins[:8] + w_ins + ins[8:]:
        copy.start()
    for copy in ins[:8]:
        copy.wait()

    for b in range(cblocks):
        part = go[:, :, b * tl : (b + 1) * tl].astype(F32)
        stage[b, 0 : channels * rows, :] = part.reshape(channels * rows, tl)
        for r in range(rows):
            line = stage[b, pl.ds(r, channels, stride=rows), :]
            tiles[r * cblocks + b] = line.astype(BF16)

    step = 8

    def forward(t, carry):
        for a in range(step):
            k = t * step + a
            product = jnp.dot(tiles[ft_s[0, k]], weights[k], preferred_element_type=F32)
            terms[pl.ds(pl.multiple_of(k * channels, channels), channels), :] = product
        return carry

    for n in range(w_chunks):
        w_ins[n].wait()
        lax.fori_loop(n * w_len // step, (n + 1) * w_len // step, forward, 0)

    def owner_parts(slot):
        owner = lax.shift_right_logical(slot * (65536 // per + 1), 16)
        place = slot - owner * per
        z = lax.shift_right_logical(owner, n1.bit_length() - 1)
        i = owner & (n1 - 1)
        return (i * n2 + z) * per + place

    live = jnp.sum(sc_v[...], axis=1, keepdims=True)
    in_use = lax.broadcasted_iota(jnp.int32, (1, nb), 1) < live
    eye = lax.broadcasted_iota(jnp.int32, (ct_all, ct_all), 0) == lax.broadcasted_iota(
        jnp.int32, (ct_all, ct_all), 1
    )
    row_of = owner_parts(os_v[...])
    column = jnp.sum(jnp.where(eye, row_of, 0), axis=1, keepdims=True)
    match = lax.broadcasted_iota(jnp.int32, (ct_all, nb), 0) == ct_v[...]
    row_of_block = jnp.sum(jnp.where(match, column, 0), axis=0, keepdims=True)
    row_of_block = jnp.where(in_use, row_of_block, -1)
    select = (lax.broadcasted_iota(jnp.int32, (ct_all, nb), 0) == row_of_block).astype(F32)
    select = jnp.concatenate([select.astype(BF16)] * 2, axis=1)

    def gather_sum(chooser, target, count):
        for c in range(0, channels, 2):
            parts = [terms[pl.ds(c + a, nb, stride=channels), :] for a in range(2)]
            high, low = split_bf16(jnp.concatenate(parts, axis=1))
            both = jnp.concatenate([high, low], axis=0)
            total = jnp.dot(chooser, both, preferred_element_type=F32)
            for a in range(2):
                target[pl.ds(c + a, count, stride=channels), :] = total[:, a * tl : (a + 1) * tl]

    gather_sum(select, sums, ct_all)
    tx1[...] = sums[...].astype(BF16).reshape(ct_all, channels, tl)

    peers = (plane_count - 1) + (n2 - 1)
    peers = peers + jnp.minimum(me, 1) + jnp.minimum(bands - 1 - me, 1)
    pl.semaphore_wait(barrier, peers)

    def remote(src, dst, send, recv, device):
        return pltpu.make_async_remote_copy(
            src_ref=src,
            dst_ref=dst,
            send_sem=send,
            recv_sem=recv,
            device_id=device,
            device_id_type=MESH,
        )

    first = []
    for e in range(1, n2 + 1):
        z = (my_o + e) % n2
        for d in range(1, n1):
            to = (my_i + d) % n1
            copy = remote(
                tx1.at[pl.ds((to * n2 + z) * per, per)],
                rx1.at[d - 1, e - 1],
                s1s.at[d - 1, e - 1],
                s1r.at[d - 1, e - 1],
                inner(to),
            )
            copy.start()
            first.append(copy)

    def transpose_weights(lo, hi):
        def body(k, carry):
            weights_t[k] = weights[k].T
            return carry

        lax.fori_loop(lo, hi, body, 0)

    ins[8].wait()
    ins[9].wait()
    for b in range(cblocks):
        part = feat[:, :, b * tl : (b + 1) * tl].astype(F32)
        stage[b] = part.reshape(cin * rows, tl)
        for r in range(rows):
            line = stage[b, pl.ds(r, cin, stride=rows), :]
            featr[r + 1, :, b * tl : (b + 1) * tl] = line.astype(BF16)

    up_dev = {"band": jnp.maximum(me - 1, 0)}
    down_dev = {"band": jnp.minimum(me + 1, bands - 1)}
    f_up = remote(featr.at[1], featr.at[rows + 1], fhs.at[0], fhr.at[1], up_dev)
    f_down = remote(featr.at[rows], featr.at[0], fhs.at[1], fhr.at[0], down_dev)

    @pl.when(me > 0)
    def _():
        f_up.start()

    @pl.when(me == 0)
    def _():
        featr[0] = jnp.zeros((cin, cols), BF16)

    @pl.when(me < bands - 1)
    def _():
        f_down.start()

    @pl.when(me == bands - 1)
    def _():
        featr[rows + 1] = jnp.zeros((cin, cols), BF16)

    fine = jnp.where(in_use, ft_v[...], -1)
    pick = (lax.broadcasted_iota(jnp.int32, (n_tiles, nb), 0) == fine).astype(F32)
    pick = jnp.concatenate([pick.astype(BF16)] * 2, axis=1)
    slab = 3 * channels
    kernel_rows = jnp.concatenate([cw[(2 - p) * slab : (3 - p) * slab, :] for p in range(3)], axis=0)
    kernel_t = kernel_rows.astype(F32).T.astype(BF16)

    size = per * channels

    def inner_sum(z, e):
        for copy in first[(e - 1) * (n1 - 1) : e * (n1 - 1)]:
            copy.wait()
        own = sums[pl.ds(pl.multiple_of((my_i * group + z * per) * channels, size), size), :]
        for d in range(n1 - 1):
            own = own + rx1[d, e - 1].astype(F32).reshape(size, tl)
        return own

    second = []
    for e in range(1, n2):
        to = (my_o + e) % n2
        tx2[e - 1] = inner_sum(to, e).astype(BF16).reshape(per, channels, tl)
        copy = remote(tx2.at[e - 1], rx2.at[e - 1], s2s.at[e - 1], s2r.at[e - 1], outer(to))
        copy.start()
        second.append(copy)
    owned = inner_sum(my_o, n2)
    transpose_weights(0, nb // 2)
    for e in range(1, n2):
        second[e - 1].wait()
        owned = owned + rx2[e - 1].astype(F32).reshape(size, tl)

    def place(i, z):
        return back.at[pl.ds((i * n2 + z) * per, per)]

    back[pl.ds((my_i * n2 + my_o) * per, per)] = owned.astype(BF16).reshape(per, channels, tl)

    sent = []

    def pass_on(z, e):
        here = place(my_i, z)
        for d in range(1, n1):
            copy = remote(
                here, here, gis.at[d - 1, e], grs.at[my_i, z], inner((my_i + d) % n1)
            )
            copy.start()
            sent.append(copy)

    mine = place(my_i, my_o)
    for e in range(1, n2):
        copy = remote(mine, mine, gos.at[e - 1], grs.at[my_i, my_o], outer((my_o + e) % n2))
        copy.start()
        sent.append(copy)
    pass_on(my_o, 0)
    co_out[...] = owned.reshape(per, channels, tl)
    transpose_weights(nb // 2, nb)
    for e in range(1, n2):
        z = (my_o + n2 - e) % n2
        here = place(my_i, z)
        remote(here, here, gos.at[e - 1], grs.at[my_i, z], outer(z)).wait_recv()
        pass_on(z, e)
    for d in range(1, n1):
        i = (my_i + d) % n1
        for e in range(n2):
            z = (my_o + n2 - e) % n2
            here = place(i, z)
            remote(here, here, gis.at[d - 1, e], grs.at[i, z], inner(i)).wait_recv()
    for copy in sent:
        copy.wait_send()

    def row_index(slot):
        owner = slot // per
        return ((owner % n1) * n2 + owner // n1) * per + slot % per

    def backward(t, carry):
        for a in range(step):
            k = t * step + a
            value = back[row_index(os_s[0, ct_s[0, k]])]
            product = jnp.dot(value, weights_t[k], preferred_element_type=F32)
            terms[pl.ds(pl.multiple_of(k * channels, channels), channels), :] = product
        return carry

    lax.fori_loop(0, nb // step, backward, 0)
    gather_sum(pick, corr, n_tiles)

    col = lax.broadcasted_iota(jnp.int32, (channels, cols), 1)

    def mid_row(r):
        parts = []
        for b in range(cblocks):
            g = r * cblocks + b
            parts.append(tiles[g].astype(F32) - corr[g * channels : (g + 1) * channels, :])
        return jnp.concatenate(parts, axis=1).astype(BF16)

    def put_row(p, line):
        wide = line.astype(F32)
        later = jnp.where(col == cols - 1, 0.0, pltpu.roll(wide, cols - 1, 1))
        earlier = jnp.where(col == 0, 0.0, pltpu.roll(wide, 1, 1))
        comb[p * slab : p * slab + channels, :] = later.astype(BF16)
        comb[p * slab + channels : p * slab + 2 * channels, :] = line
        comb[p * slab + 2 * channels : (p + 1) * slab, :] = earlier.astype(BF16)

    top, bottom = mid_row(0), mid_row(rows - 1)
    edges[0] = top
    edges[1] = bottom
    up = remote(edges.at[0], halo.at[1], hs.at[0], hr.at[1], up_dev)
    down = remote(edges.at[1], halo.at[0], hs.at[1], hr.at[0], down_dev)

    @pl.when(me > 0)
    def _():
        up.start()

    @pl.when(me < bands - 1)
    def _():
        down.start()

    put_row(1, top)
    put_row(rows, bottom)
    for r in range(1, rows - 1):
        put_row(r + 1, mid_row(r))

    @pl.when(me > 0)
    def _():
        f_down.wait_recv()
        f_up.wait_send()

    @pl.when(me < bands - 1)
    def _():
        f_up.wait_recv()
        f_down.wait_send()

    total = jnp.zeros((slab, 3 * cin), F32)
    for r in range(rows):
        near = featr[r : r + 3].reshape(3 * cin, cols)
        line = comb[(r + 1) * slab : (r + 2) * slab, :]
        total = total + lax.dot_general(line, near, NT, preferred_element_type=F32)
    total = total * scaling
    lines = ar1.shape[1]
    extra = [total[lines:, u * cin : (u + 1) * cin] for u in range(3)]
    extra.append(jnp.zeros((lines - 3 * (slab - lines), cin), F32))
    packed = jnp.concatenate([total[:lines], jnp.concatenate(extra, axis=0)], axis=1)

    def exchange(value, buf, send, recv, count, index, device):
        buf[index] = value
        copies = []
        for d in range(1, count):
            copy = remote(
                buf.at[index],
                buf.at[index],
                send.at[d - 1],
                recv.at[index],
                device((index + d) % count),
            )
            copy.start()
            copies.append(copy)

        def finish():
            for d in range(1, count):
                source = (index + d) % count
                remote(
                    buf.at[source], buf.at[source], send.at[d - 1], recv.at[source], device(source)
                ).wait_recv()
            for copy in copies:
                copy.wait_send()
            result = buf[0]
            for m in range(1, count):
                result = result + buf[m]
            return result

        return finish

    finish = exchange(packed, ar1, a1s, a1r, plane_count, my_p, plane)

    def conv_row(r):
        window = comb[r * slab : (r + 3) * slab, :]
        result = jnp.dot(kernel_t, window, preferred_element_type=F32)
        for b in range(cblocks):
            stage[b, pl.ds(r, cin, stride=rows), :] = result[:, b * tl : (b + 1) * tl]

    for r in range(1, rows - 1):
        conv_row(r)

    finish = exchange(finish(), ar2, a2s, a2r, n2, my_o, outer)

    @pl.when(me > 0)
    def _():
        down.wait_recv()
        put_row(0, halo[0])

    @pl.when(me == 0)
    def _():
        comb[0:slab, :] = jnp.zeros((slab, cols), BF16)

    @pl.when(me < bands - 1)
    def _():
        up.wait_recv()
        put_row(rows + 1, halo[1])

    @pl.when(me == bands - 1)
    def _():
        comb[(rows + 1) * slab : (rows + 2) * slab, :] = jnp.zeros((slab, cols), BF16)

    conv_row(0)
    conv_row(rows - 1)
    for b in range(cblocks):
        part = stage[b].reshape(cin, rows, tl)
        gf_out[:, :, b * tl : (b + 1) * tl] = part.astype(BF16)
    packed = finish()
    rest = slab - lines
    for u in range(3):
        cg_out[u * slab : u * slab + lines, :] = packed[:, u * cin : (u + 1) * cin]
        cg_out[u * slab + lines : (u + 1) * slab, :] = packed[u * rest : (u + 1) * rest, 3 * cin :]

    @pl.when(me > 0)
    def _():
        up.wait_send()

    @pl.when(me < bands - 1)
    def _():
        down.wait_send()


def write_out(gf_in, cg_in, co_in, gf_out, cg_out, co_out, sems):
    pairs = ((gf_in, gf_out), (cg_in, cg_out), (co_in, co_out))
    copies = [pltpu.make_async_copy(a, b, sems.at[n]) for n, (a, b) in enumerate(pairs)]
    for copy in copies:
        copy.start()
    for copy in copies:
        copy.wait()


def per_device(
    n_dp,
    bands,
    grad_out,
    features,
    conv_weight,
    block_weights,
    fine_tile,
    coarse_tile,
    owner_slot,
    send_counts,
):
    channels, rows, cols = grad_out.shape[1:]
    cin = features.shape[1]
    nb, tl = block_weights.shape[:2]
    ct_all = owner_slot.shape[0]
    per = ct_all // bands
    n1 = 4
    n2 = bands // n1
    n_tiles = rows * cols // tl
    scaling = 1.0 / math.sqrt(n_dp * bands * rows * cols)
    dims = (n_dp, bands, n1, n2, channels, cin, rows, cols, tl, nb, per, ct_all, scaling)
    slab = 3 * channels
    lines = slab - 8
    w_chunks = 4
    dma = pltpu.SemaphoreType.DMA
    vmem = pl.BlockSpec(memory_space=pltpu.VMEM)
    gf, cg, co = pl.pallas_call(
        functools.partial(kernel, dims),
        out_shape=(
            jax.ShapeDtypeStruct((cin, rows, cols), BF16),
            jax.ShapeDtypeStruct((3 * slab, cin), F32),
            jax.ShapeDtypeStruct((per, channels, tl), F32),
        ),
        in_specs=[pl.BlockSpec(memory_space=pltpu.HBM)] * 8,
        out_specs=(vmem, vmem, vmem),
        scratch_shapes=[
            pltpu.VMEM((cols // tl, cin * rows, tl), F32),
            pltpu.VMEM((n_tiles, channels, tl), BF16),
            pltpu.VMEM((nb * channels, tl), F32),
            pltpu.VMEM((ct_all * channels, tl), F32),
            pltpu.VMEM((ct_all, channels, tl), BF16),
            pltpu.VMEM((n1 - 1, n2, per, channels, tl), BF16),
            pltpu.VMEM((n2 - 1, per, channels, tl), BF16),
            pltpu.VMEM((n2 - 1, per, channels, tl), BF16),
            pltpu.VMEM((ct_all, channels, tl), BF16),
            pltpu.VMEM((n_tiles * channels, tl), F32),
            pltpu.VMEM(((rows + 2) * slab, cols), BF16),
            pltpu.VMEM((rows + 2, cin, cols), BF16),
            pltpu.VMEM((2, channels, cols), BF16),
            pltpu.VMEM((2, channels, cols), BF16),
            pltpu.VMEM((n1 * n_dp, lines, 4 * cin), F32),
            pltpu.VMEM((n2, lines, 4 * cin), F32),
            pltpu.VMEM((nb, tl, tl), BF16),
            pltpu.VMEM((nb, tl, tl), BF16),
            pltpu.VMEM((channels, rows, cols), BF16),
            pltpu.VMEM((cin, rows, cols), BF16),
            pltpu.VMEM((3 * slab, cin), BF16),
            pltpu.SMEM((1, nb), jnp.int32),
            pltpu.SMEM((1, nb), jnp.int32),
            pltpu.SMEM((1, ct_all), jnp.int32),
            pltpu.VMEM((1, nb), jnp.int32),
            pltpu.VMEM((1, nb), jnp.int32),
            pltpu.VMEM((1, ct_all), jnp.int32),
            pltpu.VMEM((1, bands), jnp.int32),
            dma((10,)),
            dma((w_chunks,)),
            dma((2,)),
            dma((2,)),
            dma((n1 - 1, n2)),
            dma((n1 - 1, n2)),
            dma((n2 - 1,)),
            dma((n2 - 1,)),
            dma((n2 - 1,)),
            dma((n1 - 1, n2)),
            dma((n1, n2)),
            dma((2,)),
            dma((2,)),
            dma((n1 * n_dp - 1,)),
            dma((n1 * n_dp,)),
            dma((n2 - 1,)),
            dma((n2,)),
        ],
        compiler_params=pltpu.CompilerParams(
            collective_id=0, has_side_effects=True, vmem_limit_bytes=64 * 1024 * 1024
        ),
    )(
        fine_tile.reshape(1, nb),
        coarse_tile.reshape(1, nb),
        owner_slot.reshape(1, ct_all),
        send_counts,
        grad_out.reshape(channels, rows, cols),
        features.reshape(cin, rows, cols),
        conv_weight.reshape(3 * slab, cin),
        block_weights,
    )
    hbm = pl.BlockSpec(memory_space=pltpu.HBM)
    gf, cg, co = pl.pallas_call(
        write_out,
        out_shape=tuple(jax.ShapeDtypeStruct(x.shape, x.dtype) for x in (gf, cg, co)),
        in_specs=[pl.BlockSpec(memory_space=pl.ANY)] * 3,
        out_specs=(hbm,) * 3,
        scratch_shapes=[dma((3,))],
    )(gf, cg, co)
    return gf[None], cg.reshape(3, 3, channels, cin), co[None]


def solution(mesh):
    placed = (
        P("dp", None, "band", None),
        P("dp", None, "band", None),
        P(),
        P("band", None, None),
        P("band"),
        P("band"),
        P(),
        P("band", None),
    )
    return jax.shard_map(
        functools.partial(per_device, mesh.shape["dp"], mesh.shape["band"]),
        mesh=mesh,
        in_specs=placed,
        out_specs=(P("dp", None, "band", None), P(), P("dp", "band", None, None)),
        check_vma=False,
    )
```

```python
import functools
import math

import jax
import jax.numpy as jnp
from jax import lax
from jax.experimental import pallas as pl
from jax.experimental.pallas import tpu as pltpu
from jax.sharding import PartitionSpec as P

F32 = jnp.float32
BF16 = jnp.bfloat16
MESH = pl.DeviceIdType.MESH
NT = (((1,), (1,)), ((), ()))


def split_bf16(value):
    high = value.astype(BF16)
    low = (value - high.astype(F32)).astype(BF16)
    return high, low


def kernel(
    dims,
    ft_h,
    ct_h,
    os_h,
    sc_h,
    go_h,
    feat_h,
    cw_h,
    weights_h,
    gf_out,
    cg_out,
    co_out,
    stage,
    tiles,
    terms,
    sums,
    tx1,
    rx1,
    tx2,
    rx2,
    back,
    corr,
    comb,
    featr,
    edges,
    halo,
    ar0,
    ar1,
    ar2,
    ar3,
    weights,
    go,
    feat,
    cw,
    ft_s,
    ct_s,
    os_s,
    ft_v,
    ct_v,
    os_v,
    sc_v,
    loads,
    wloads,
    fhs,
    fhr,
    s1s,
    s1r,
    s2s,
    s2r,
    gos,
    gis,
    grs,
    hs,
    hr,
    a1s,
    a1r,
    a2s,
    a2r,
    a3s,
    a3r,
):
    n_dp, bands, n1, n2, channels, cin, rows, cols, tl, nb, per, ct_all, scaling = dims
    cblocks = cols // tl
    n_tiles = rows * cblocks
    group = n2 * per
    me = lax.axis_index("band")
    my_dp = lax.axis_index("dp")
    my_o = me // n1
    my_i = me % n1

    barrier = pltpu.get_barrier_semaphore()

    def inner(i):
        return {"band": my_o * n1 + i}

    def outer(z):
        return {"band": z * n1 + my_i}

    def greet(device):
        pl.semaphore_signal(barrier, inc=1, device_id=device, device_id_type=MESH)

    plane_count = n1 * n_dp
    my_p = my_dp * n1 + my_i

    def plane(p):
        return {"dp": p // n1, "band": my_o * n1 + p % n1}

    for d in range(1, plane_count):
        greet(plane((my_p + d) % plane_count))
    for e in range(1, n2):
        greet(outer((my_o + e) % n2))

    @pl.when(me > 0)
    def _():
        greet({"band": me - 1})

    @pl.when(me < bands - 1)
    def _():
        greet({"band": me + 1})

    ins = []
    for n, (src, dst) in enumerate(
        [
            (go_h, go),
            (ft_h, ft_s),
            (ct_h, ct_s),
            (os_h, os_s),
            (ft_h, ft_v),
            (ct_h, ct_v),
            (os_h, os_v),
            (sc_h, sc_v),
            (feat_h, feat),
            (cw_h, cw),
        ]
    ):
        ins.append(pltpu.make_async_copy(src, dst, loads.at[n]))
    w_chunks = wloads.shape[0]
    w_len = nb // w_chunks
    w_ins = [
        pltpu.make_async_copy(
            weights_h.at[pl.ds(n * w_len, w_len)], weights.at[pl.ds(n * w_len, w_len)], wloads.at[n]
        )
        for n in range(w_chunks)
    ]
    for copy in ins[:8] + w_ins + ins[8:]:
        copy.start()
    for copy in ins[:8]:
        copy.wait()

    for b in range(cblocks):
        part = go[:, :, b * tl : (b + 1) * tl].astype(F32)
        stage[b, 0 : channels * rows, :] = part.reshape(channels * rows, tl)
        for r in range(rows):
            line = stage[b, pl.ds(r, channels, stride=rows), :]
            tiles[r * cblocks + b] = line.astype(BF16)

    step = 8

    def forward(t, carry):
        for a in range(step):
            k = t * step + a
            product = jnp.dot(tiles[ft_s[0, k]], weights[k], preferred_element_type=F32)
            terms[pl.ds(pl.multiple_of(k * channels, channels), channels), :] = product
        return carry

    for n in range(w_chunks):
        w_ins[n].wait()
        lax.fori_loop(n * w_len // step, (n + 1) * w_len // step, forward, 0)

    def owner_parts(slot):
        owner = lax.shift_right_logical(slot * (65536 // per + 1), 16)
        place = slot - owner * per
        z = lax.shift_right_logical(owner, n1.bit_length() - 1)
        i = owner & (n1 - 1)
        return (i * n2 + z) * per + place

    live = jnp.sum(sc_v[...], axis=1, keepdims=True)
    in_use = lax.broadcasted_iota(jnp.int32, (1, nb), 1) < live
    eye = lax.broadcasted_iota(jnp.int32, (ct_all, ct_all), 0) == lax.broadcasted_iota(
        jnp.int32, (ct_all, ct_all), 1
    )
    row_of = owner_parts(os_v[...])
    column = jnp.sum(jnp.where(eye, row_of, 0), axis=1, keepdims=True)
    match = lax.broadcasted_iota(jnp.int32, (ct_all, nb), 0) == ct_v[...]
    row_of_block = jnp.sum(jnp.where(match, column, 0), axis=0, keepdims=True)
    row_of_block = jnp.where(in_use, row_of_block, -1)
    select = (lax.broadcasted_iota(jnp.int32, (ct_all, nb), 0) == row_of_block).astype(F32)
    select = jnp.concatenate([select.astype(BF16)] * 2, axis=1)

    def gather_sum(chooser, target, count):
        for c in range(0, channels, 2):
            parts = [terms[pl.ds(c + a, nb, stride=channels), :] for a in range(2)]
            high, low = split_bf16(jnp.concatenate(parts, axis=1))
            both = jnp.concatenate([high, low], axis=0)
            total = jnp.dot(chooser, both, preferred_element_type=F32)
            for a in range(2):
                target[pl.ds(c + a, count, stride=channels), :] = total[:, a * tl : (a + 1) * tl]

    gather_sum(select, sums, ct_all)
    tx1[...] = sums[...].astype(BF16).reshape(ct_all, channels, tl)

    peers = (plane_count - 1) + (n2 - 1)
    peers = peers + jnp.minimum(me, 1) + jnp.minimum(bands - 1 - me, 1)
    pl.semaphore_wait(barrier, peers)

    def remote(src, dst, send, recv, device):
        return pltpu.make_async_remote_copy(
            src_ref=src,
            dst_ref=dst,
            send_sem=send,
            recv_sem=recv,
            device_id=device,
            device_id_type=MESH,
        )

    first = []
    for e in range(1, n2 + 1):
        z = (my_o + e) % n2
        for d in range(1, n1):
            to = (my_i + d) % n1
            copy = remote(
                tx1.at[pl.ds((to * n2 + z) * per, per)],
                rx1.at[d - 1, e - 1],
                s1s.at[d - 1, e - 1],
                s1r.at[d - 1, e - 1],
                inner(to),
            )
            copy.start()
            first.append(copy)

    ins[8].wait()
    ins[9].wait()
    for b in range(cblocks):
        part = feat[:, :, b * tl : (b + 1) * tl].astype(F32)
        stage[b] = part.reshape(cin * rows, tl)
        for r in range(rows):
            line = stage[b, pl.ds(r, cin, stride=rows), :]
            featr[r + 1, :, b * tl : (b + 1) * tl] = line.astype(BF16)

    up_dev = {"band": jnp.maximum(me - 1, 0)}
    down_dev = {"band": jnp.minimum(me + 1, bands - 1)}
    f_up = remote(featr.at[1], featr.at[rows + 1], fhs.at[0], fhr.at[1], up_dev)
    f_down = remote(featr.at[rows], featr.at[0], fhs.at[1], fhr.at[0], down_dev)

    @pl.when(me > 0)
    def _():
        f_up.start()

    @pl.when(me == 0)
    def _():
        featr[0] = jnp.zeros((cin, cols), BF16)

    @pl.when(me < bands - 1)
    def _():
        f_down.start()

    @pl.when(me == bands - 1)
    def _():
        featr[rows + 1] = jnp.zeros((cin, cols), BF16)

    fine = jnp.where(in_use, ft_v[...], -1)
    pick = (lax.broadcasted_iota(jnp.int32, (n_tiles, nb), 0) == fine).astype(F32)
    pick = jnp.concatenate([pick.astype(BF16)] * 2, axis=1)
    slab = 3 * channels
    kernel_rows = jnp.concatenate([cw[(2 - p) * slab : (3 - p) * slab, :] for p in range(3)], axis=0)
    kernel_t = kernel_rows.astype(F32).T.astype(BF16)

    size = per * channels

    def inner_sum(z, e):
        for copy in first[(e - 1) * (n1 - 1) : e * (n1 - 1)]:
            copy.wait()
        own = sums[pl.ds(pl.multiple_of((my_i * group + z * per) * channels, size), size), :]
        for d in range(n1 - 1):
            own = own + rx1[d, e - 1].astype(F32).reshape(size, tl)
        return own

    second = []
    for e in range(1, n2):
        to = (my_o + e) % n2
        tx2[e - 1] = inner_sum(to, e).astype(BF16).reshape(per, channels, tl)
        copy = remote(tx2.at[e - 1], rx2.at[e - 1], s2s.at[e - 1], s2r.at[e - 1], outer(to))
        copy.start()
        second.append(copy)
    owned = inner_sum(my_o, n2)
    for e in range(1, n2):
        second[e - 1].wait()
        owned = owned + rx2[e - 1].astype(F32).reshape(size, tl)

    def place(i, z):
        return back.at[pl.ds((i * n2 + z) * per, per)]

    back[pl.ds((my_i * n2 + my_o) * per, per)] = owned.astype(BF16).reshape(per, channels, tl)

    sent = []

    side = my_i + 1 - 2 * (my_i % 2)
    across = (my_i + 2) % n1
    corner = (side + 2) % n1

    def hand(i, z, send, device):
        here = place(i, z)
        copy = remote(here, here, send, grs.at[i, z], device)
        copy.start()
        sent.append(copy)

    def take(i, z, send, device):
        here = place(i, z)
        remote(here, here, send, grs.at[i, z], device).wait_recv()

    def pass_on(z, e):
        hand(my_i, z, gis.at[0, e], inner(across))
        hand(my_i, z, gis.at[1, e], inner(side))

    for e in range(1, n2):
        hand(my_i, my_o, gos.at[e - 1], outer((my_o + e) % n2))
    pass_on(my_o, 0)
    co_out[...] = owned.reshape(per, channels, tl)
    for e in range(n2):
        z = (my_o + n2 - e) % n2
        if e > 0:
            take(my_i, z, gos.at[e - 1], outer(z))
            pass_on(z, e)
        if e > 0:
            zp = (my_o + n2 - e + 1) % n2
            take(across, zp, gis.at[0, e - 1], inner(across))
            hand(across, zp, gis.at[2, e - 1], inner(side))
    zp = (my_o + 1) % n2
    take(across, zp, gis.at[0, n2 - 1], inner(across))
    hand(across, zp, gis.at[2, n2 - 1], inner(side))
    for e in range(n2):
        z = (my_o + n2 - e) % n2
        take(side, z, gis.at[1, e], inner(side))
        take(corner, z, gis.at[2, e], inner(side))
    for copy in sent:
        copy.wait_send()

    def row_index(slot):
        owner = slot // per
        return ((owner % n1) * n2 + owner // n1) * per + slot % per

    def backward(t, carry):
        for a in range(step):
            k = t * step + a
            value = back[row_index(os_s[0, ct_s[0, k]])]
            product = lax.dot_general(value, weights[k], NT, preferred_element_type=F32)
            terms[pl.ds(pl.multiple_of(k * channels, channels), channels), :] = product
        return carry

    lax.fori_loop(0, nb // step, backward, 0)
    gather_sum(pick, corr, n_tiles)

    col = lax.broadcasted_iota(jnp.int32, (channels, cols), 1)

    def mid_row(r):
        parts = []
        for b in range(cblocks):
            g = r * cblocks + b
            parts.append(tiles[g].astype(F32) - corr[g * channels : (g + 1) * channels, :])
        return jnp.concatenate(parts, axis=1).astype(BF16)

    def put_row(p, line):
        wide = line.astype(F32)
        later = jnp.where(col == cols - 1, 0.0, pltpu.roll(wide, cols - 1, 1))
        earlier = jnp.where(col == 0, 0.0, pltpu.roll(wide, 1, 1))
        comb[p * slab : p * slab + channels, :] = later.astype(BF16)
        comb[p * slab + channels : p * slab + 2 * channels, :] = line
        comb[p * slab + 2 * channels : (p + 1) * slab, :] = earlier.astype(BF16)

    top, bottom = mid_row(0), mid_row(rows - 1)
    edges[0] = top
    edges[1] = bottom
    up = remote(edges.at[0], halo.at[1], hs.at[0], hr.at[1], up_dev)
    down = remote(edges.at[1], halo.at[0], hs.at[1], hr.at[0], down_dev)

    @pl.when(me > 0)
    def _():
        up.start()

    @pl.when(me < bands - 1)
    def _():
        down.start()

    put_row(1, top)
    put_row(rows, bottom)
    for r in range(1, rows - 1):
        put_row(r + 1, mid_row(r))

    @pl.when(me > 0)
    def _():
        f_down.wait_recv()
        f_up.wait_send()

    @pl.when(me < bands - 1)
    def _():
        f_up.wait_recv()
        f_down.wait_send()

    total = jnp.zeros((slab, 3 * cin), F32)
    for r in range(rows):
        near = featr[r : r + 3].reshape(3 * cin, cols)
        line = comb[(r + 1) * slab : (r + 2) * slab, :]
        total = total + lax.dot_general(line, near, NT, preferred_element_type=F32)
    total = total * scaling
    total = jnp.concatenate([total, jnp.zeros((slab, cin), F32)], axis=1)
    ar0[...] = jnp.zeros(ar0.shape, F32)
    ar0[0 : slab // 8] = total.reshape(slab // 8, 8, 4 * cin)
    ar1[my_p] = ar0[my_p]
    scatter = []
    for d in range(1, plane_count):
        to = (my_p + d) % plane_count
        copy = remote(ar0.at[to], ar1.at[my_p], a1s.at[d - 1], a1r.at[my_p], plane(to))
        copy.start()
        scatter.append(copy)

    def exchange(value, buf, send, recv, count, index, device, summed):
        buf[index] = value
        copies = []
        for d in range(1, count):
            copy = remote(
                buf.at[index],
                buf.at[index],
                send.at[d - 1],
                recv.at[index],
                device((index + d) % count),
            )
            copy.start()
            copies.append(copy)

        def finish():
            for d in range(1, count):
                source = (index + d) % count
                remote(
                    buf.at[source], buf.at[source], send.at[d - 1], recv.at[source], device(source)
                ).wait_recv()
            for copy in copies:
                copy.wait_send()
            if not summed:
                return None
            result = buf[0]
            for m in range(1, count):
                result = result + buf[m]
            return result

        return finish

    def conv_row(r):
        window = comb[r * slab : (r + 3) * slab, :]
        result = jnp.dot(kernel_t, window, preferred_element_type=F32)
        for b in range(cblocks):
            stage[b, pl.ds(r, cin, stride=rows), :] = result[:, b * tl : (b + 1) * tl]

    half = rows // 2
    for r in range(1, half):
        conv_row(r)

    for d in range(1, plane_count):
        source = (my_p + d) % plane_count
        remote(
            ar0.at[source], ar1.at[source], a1s.at[d - 1], a1r.at[source], plane(source)
        ).wait_recv()
    for copy in scatter:
        copy.wait_send()
    share = ar1[0]
    for m in range(1, plane_count):
        share = share + ar1[m]
    finish = exchange(share, ar2, a2s, a2r, n2, my_o, outer, True)
    for r in range(half, rows - 1):
        conv_row(r)

    finish = exchange(finish(), ar3, a3s, a3r, plane_count, my_p, plane, False)

    @pl.when(me > 0)
    def _():
        down.wait_recv()
        put_row(0, halo[0])

    @pl.when(me == 0)
    def _():
        comb[0:slab, :] = jnp.zeros((slab, cols), BF16)

    @pl.when(me < bands - 1)
    def _():
        up.wait_recv()
        put_row(rows + 1, halo[1])

    @pl.when(me == bands - 1)
    def _():
        comb[(rows + 1) * slab : (rows + 2) * slab, :] = jnp.zeros((slab, cols), BF16)

    conv_row(0)
    conv_row(rows - 1)
    for b in range(cblocks):
        part = stage[b].reshape(cin, rows, tl)
        gf_out[:, :, b * tl : (b + 1) * tl] = part.astype(BF16)
    finish()
    total = ar3[0 : slab // 8].reshape(slab, 4 * cin)
    for u in range(3):
        cg_out[u * slab : (u + 1) * slab, :] = total[:, u * cin : (u + 1) * cin]

    @pl.when(me > 0)
    def _():
        up.wait_send()

    @pl.when(me < bands - 1)
    def _():
        down.wait_send()


def write_out(gf_in, cg_in, co_in, gf_out, cg_out, co_out):
    gf_out[...] = gf_in[...]
    cg_out[...] = cg_in[...]
    co_out[...] = co_in[...]


def per_device(
    n_dp,
    bands,
    grad_out,
    features,
    conv_weight,
    block_weights,
    fine_tile,
    coarse_tile,
    owner_slot,
    send_counts,
):
    channels, rows, cols = grad_out.shape[1:]
    cin = features.shape[1]
    nb, tl = block_weights.shape[:2]
    ct_all = owner_slot.shape[0]
    per = ct_all // bands
    n1 = 4
    n2 = bands // n1
    n_tiles = rows * cols // tl
    scaling = 1.0 / math.sqrt(n_dp * bands * rows * cols)
    dims = (n_dp, bands, n1, n2, channels, cin, rows, cols, tl, nb, per, ct_all, scaling)
    slab = 3 * channels
    members = n1 * n_dp
    w_chunks = 4
    dma = pltpu.SemaphoreType.DMA
    vmem = pl.BlockSpec(memory_space=pltpu.VMEM)
    gf, cg, co = pl.pallas_call(
        functools.partial(kernel, dims),
        out_shape=(
            jax.ShapeDtypeStruct((cin, rows, cols), BF16),
            jax.ShapeDtypeStruct((3 * slab, cin), F32),
            jax.ShapeDtypeStruct((per, channels, tl), F32),
        ),
        in_specs=[pl.BlockSpec(memory_space=pltpu.HBM)] * 8,
        out_specs=(vmem, vmem, vmem),
        scratch_shapes=[
            pltpu.VMEM((cols // tl, cin * rows, tl), F32),
            pltpu.VMEM((n_tiles, channels, tl), BF16),
            pltpu.VMEM((nb * channels, tl), F32),
            pltpu.VMEM((ct_all * channels, tl), F32),
            pltpu.VMEM((ct_all, channels, tl), BF16),
            pltpu.VMEM((n1 - 1, n2, per, channels, tl), BF16),
            pltpu.VMEM((n2 - 1, per, channels, tl), BF16),
            pltpu.VMEM((n2 - 1, per, channels, tl), BF16),
            pltpu.VMEM((ct_all, channels, tl), BF16),
            pltpu.VMEM((n_tiles * channels, tl), F32),
            pltpu.VMEM(((rows + 2) * slab, cols), BF16),
            pltpu.VMEM((rows + 2, cin, cols), BF16),
            pltpu.VMEM((2, channels, cols), BF16),
            pltpu.VMEM((2, channels, cols), BF16),
            pltpu.VMEM((members, 8, 4 * cin), F32),
            pltpu.VMEM((members, 8, 4 * cin), F32),
            pltpu.VMEM((n2, 8, 4 * cin), F32),
            pltpu.VMEM((members, 8, 4 * cin), F32),
            pltpu.VMEM((nb, tl, tl), BF16),
            pltpu.VMEM((channels, rows, cols), BF16),
            pltpu.VMEM((cin, rows, cols), BF16),
            pltpu.VMEM((3 * slab, cin), BF16),
            pltpu.SMEM((1, nb), jnp.int32),
            pltpu.SMEM((1, nb), jnp.int32),
            pltpu.SMEM((1, ct_all), jnp.int32),
            pltpu.VMEM((1, nb), jnp.int32),
            pltpu.VMEM((1, nb), jnp.int32),
            pltpu.VMEM((1, ct_all), jnp.int32),
            pltpu.VMEM((1, bands), jnp.int32),
            dma((10,)),
            dma((w_chunks,)),
            dma((2,)),
            dma((2,)),
            dma((n1 - 1, n2)),
            dma((n1 - 1, n2)),
            dma((n2 - 1,)),
            dma((n2 - 1,)),
            dma((n2 - 1,)),
            dma((n1 - 1, n2)),
            dma((n1, n2)),
            dma((2,)),
            dma((2,)),
            dma((n1 * n_dp - 1,)),
            dma((n1 * n_dp,)),
            dma((n2 - 1,)),
            dma((n2,)),
            dma((members - 1,)),
            dma((members,)),
        ],
        compiler_params=pltpu.CompilerParams(
            collective_id=0, has_side_effects=True, vmem_limit_bytes=64 * 1024 * 1024
        ),
    )(
        fine_tile.reshape(1, nb),
        coarse_tile.reshape(1, nb),
        owner_slot.reshape(1, ct_all),
        send_counts,
        grad_out.reshape(channels, rows, cols),
        features.reshape(cin, rows, cols),
        conv_weight.reshape(3 * slab, cin),
        block_weights,
    )
    gf, cg, co = pl.pallas_call(
        write_out,
        out_shape=tuple(jax.ShapeDtypeStruct(x.shape, x.dtype) for x in (gf, cg, co)),
        in_specs=[vmem] * 3,
        out_specs=(vmem,) * 3,
    )(gf, cg, co)
    return gf[None], cg.reshape(3, 3, channels, cin), co[None]


def solution(mesh):
    placed = (
        P("dp", None, "band", None),
        P("dp", None, "band", None),
        P(),
        P("band", None, None),
        P("band"),
        P("band"),
        P(),
        P("band", None),
    )
    return jax.shard_map(
        functools.partial(per_device, mesh.shape["dp"], mesh.shape["band"]),
        mesh=mesh,
        in_specs=placed,
        out_specs=(P("dp", None, "band", None), P(), P("dp", "band", None, None)),
        check_vma=False,
    )
```
